32 devices in a mesh: wide: 16 (over z, x, core), narrow: 2 (over y).
Axes of the slice: x: 2, y: 2, z: 4, core: 2. Of those that a mesh axis runs over, the one named last changes fastest.
Arguments:
- tokens: bfloat16 [2048, 2048], P('wide'), may hold values from -6 to 6
- request_lengths: int32 [16, 3], replicated, may hold values from 1 to 64, 128 in all within a row
- w_qkv: bfloat16 [2048, 3, 2048], P(None, None, 'narrow'), may hold values from -0.19921875 to 0.19921875
- qk_gain: float32 [2, 2048], P(None, 'narrow'), may hold values from 0.5 to 7
- w_out: bfloat16 [2048, 2048], P('narrow'), may hold values from -0.125 to 0.125
- norm_gains: float32 [3, 2048], replicated, may hold values from 0.25 to 1.75
- w_router: bfloat16 [2048, 32], replicated, may hold values from -0.0625 to 0.0625
- routes: int32 [2048, 8], P('wide'), may hold values from 0 to 31, all different within a row; in each aligned block of 128 rows (0 to 127, 128 to 255, ...) at most 40 rows name the same one
- w_gate: bfloat16 [32, 2048, 1024], P('wide', None, 'narrow'), may hold values from -0.125 to 0.125
- w_up: bfloat16 [32, 2048, 1024], P('wide', None, 'narrow'), may hold values from -0.125 to 0.125
- w_down: bfloat16 [32, 1024, 2048], P('wide', 'narrow'), may hold values from -0.1875 to 0.1875
- w_proj: bfloat16 [2048, 128], replicated, may hold values from -0.125 to 0.125
- doc_vectors: bfloat16 [32768, 128], P(('wide', 'narrow')), may hold values from -6 to 6
- doc_segment: int32 [32, 1024], P(('wide', 'narrow')), may hold values from 0 to 15, never falling along the last dimension, each value on 1 to 128 neighbouring positions
- doc_request: int32 [32, 16], P(('wide', 'narrow')), may hold values from 0 to 47
Outputs:
- layer_out: bfloat16 [2048, 2048], P('wide')
- doc_scores: float32 [32, 16], P(('wide', 'narrow'))
The draws below stay inside these ranges and needn't reach their ends.
Inputs may be any that keep to these rules, and one draw needn't show every extreme that they name: `request_lengths`: each row sums to 128, and its largest entry is exactly 64. `routes`: each row names 8 different experts. In the rows of one index of wide (aligned blocks of 128 rows) no expert is named by more than 40 rows, a bound that some block reaches. `doc_segment`: in each row the numbers never fall, every document has one or more rows, and one document has exactly 128.
All inputs are finite; a program needn't handle non-finite values.
Results may differ from the reference program's by a relative error of at most 0.009.
Values may be sent and summed in bfloat16 or wider, within the bound.
A program may use at most 128 MiB of HBM per device.

```python
import math
import jax
import jax.numpy as jnp
import numpy as np
from jax import lax

D = 2048
HEADS = 16
HD = 128
FF = 1024
TOPK = 8
EMB = 128
TOK_DEV = 128
REQ_DEV = 3
DOCS_DEV = 16
DOC_MOST = 128
EXPERTS = 32
SHARDS = 16
TOKENS = 2048
REQUESTS = 48
MOST_REQ = 64
CAP = 40
DOC_TOK = 1024
HOLDERS = 32
N_NARROW = 2


LIMIT = 0.19921875


def draw_tokens(key, part):
    values = jax.random.normal(key, (TOKENS, D), jnp.float32)
    return jnp.clip(values, -6.0, 6.0).astype(jnp.bfloat16)


def draw_w_qkv(key, part):
    std = D ** (-0.5)
    query = jax.random.normal(jax.random.fold_in(key, 1), (D, 1, D), jnp.float32) * std
    value = jax.random.normal(jax.random.fold_in(key, 3), (D, 1, D), jnp.float32) * std
    keyed = jax.random.normal(jax.random.fold_in(key, 2), (D, 1, D), jnp.float32) * std
    return jnp.clip(jnp.concatenate([query, keyed, value], axis=1), -LIMIT, LIMIT).astype(jnp.bfloat16)


def draw_qk_gain(key, part):
    gains = jax.random.uniform(key, (2, HEADS, HD), jnp.float32, 0.6, 1.6)
    return gains.reshape(2, D)


def touch_ends(result, key, least, largest):
    longest = result.shape.index(max(result.shape))
    spots = []
    for shift in (0, 1):
        where = [jax.random.randint(jax.random.fold_in(key, axis), (), 0, length) for axis, length in enumerate(result.shape)]
        where[longest] = (where[longest] + shift) % result.shape[longest]
        spots.append(tuple(where))
    return result.at[spots[0]].set(least).at[spots[1]].set(largest)


def steps_of(stream_key, extent, pieces, low, top_value):
    def one(dim, blocks):
        heights = jax.random.uniform(jax.random.fold_in(jax.random.fold_in(stream_key, 6), dim), (blocks,), jnp.float32, low / len(pieces), top_value / len(pieces))
        return jnp.repeat(jnp.exp(heights), extent[dim] // blocks).reshape((-1,) + (1,) * (len(extent) - dim - 1))

    level = one(*pieces[0])
    for cut in pieces[1:]:
        level = level * one(*cut)
    return level


def split_up(amount, total, reach, slope):
    loads = [(1 << 20) // math.isqrt(standing ** slope) + 1 for standing in range(2, amount + 1)]
    rest, given = total - reach - (amount - 1), [1] * (amount - 1)
    while rest > 0:
        candidates = [i for i in range(amount - 1) if given[i] < reach]
        mass, remaining = sum([loads[i] for i in candidates]), rest
        for i in candidates:
            addition = min(reach - given[i], max(1, remaining * loads[i] // mass), rest)
            given[i] = given[i] + addition
            rest = rest - addition
    return np.array([reach] + given)


def ragged_sizes(key, amount, total, most, slope):
    if amount == 2:
        one = jax.random.randint(key, (), max(1, total - most), min(most, total - 1) + 1)
        return jnp.stack([one, total - one])
    lengths = jnp.asarray(split_up(amount, total, most, slope), jnp.int32)
    couples = (amount - 1) // 2
    source_of, sink = lengths[1:1 + 2 * couples:2], lengths[2:2 + 2 * couples:2]
    margin = jnp.minimum(source_of - 1, most - sink)
    passed = jax.random.randint(jax.random.fold_in(key, 1), (couples,), 0, 1 << 20) % (margin + 1)
    lengths = lengths.at[1:1 + 2 * couples:2].set(source_of - passed).at[2:2 + 2 * couples:2].set(sink + passed)
    return lengths[jax.random.permutation(jax.random.fold_in(key, 2), amount)]


def deal_out(stream_key, own, number, rows, amount, top, most, slope):
    ranking = jax.random.permutation(stream_key, amount)
    heavy_load, usual = shares(amount, rows * top, most, slope, True), shares(amount, rows * top, most, slope, False)
    places = jnp.arange(amount)

    def named(tallies, rotation):
        used = int((tallies > 0).sum())
        fixed = max(1, used // 4)
        passed = fixed + (places - fixed + rotation * (used - fixed)) % max(1, amount - fixed)
        return jnp.zeros((amount,), jnp.int32).at[ranking[jnp.where(places < fixed, places, passed)]].set(jnp.asarray(tallies, jnp.int32))

    tallies = jnp.where(number % 4 == 0, named(heavy_load, number // 4), named(usual, number - number // 4 - 1))
    mixed = jax.random.permutation(jax.random.fold_in(own, 3), amount)
    source_of, taker = mixed[0:amount // 2 * 2:2], mixed[1:amount // 2 * 2:2]
    room = jnp.minimum(tallies[source_of] - 1, most - tallies[taker]) // 2
    room = jnp.where((source_of == ranking[0]) | (taker == ranking[0]) | (tallies[taker] == 0), 0, jnp.maximum(room, 0))
    passed = jax.random.randint(jax.random.fold_in(own, 4), (amount // 2,), 0, 1 << 20) % (room + 1)
    tallies = tallies.at[source_of].add(-passed).at[taker].add(passed)
    members = jnp.searchsorted(jnp.cumsum(tallies), jnp.arange(rows * top), side="right").astype(jnp.int32)
    table = members.reshape(top, rows).T
    table = table[jax.random.permutation(jax.random.fold_in(own, 1), rows)]
    rotation = jax.random.randint(jax.random.fold_in(own, 2), (rows, 1), 0, top)
    return jnp.take_along_axis(table, (jnp.arange(top)[None, :] + rotation) % top, axis=1)


def shares(amount, total, most, skew, full):
    weights = [(1 << 20) // math.isqrt(standing ** skew) + 1 for standing in range(1, amount + 1)]
    largest = most if full else min(most, max(-(-total // amount), total * weights[0] // sum(weights)))
    least = 1 if total - largest >= amount - 1 else 0
    given, spare = [largest] + [least] * (amount - 1), total - largest - least * (amount - 1)
    while spare > 0:
        movable = [i for i in range(1, amount) if given[i] < largest] or [i for i in range(1, amount) if given[i] < most]
        pool, remaining = sum([weights[i] for i in movable]), spare
        for i in movable:
            more = min(most - given[i], max(1, remaining * weights[i] // pool), spare)
            given[i] = given[i] + more
            spare = spare - more
    return np.array(given)


def centred(key, shape, width, reach, cuts=(), kind=jnp.bfloat16):
    result = width * jax.random.normal(key, shape, jnp.float32)
    if cuts:
        result = result * steps_of(key, shape, cuts, -0.22, 0.18)
    return jnp.clip(result, -reach, reach).astype(kind)


def setup_inputs(seed: int = 0) -> dict:
    key_of = jax.random.split(jax.random.key(seed), 16)
    tokens = draw_tokens(jax.random.fold_in(key_of[15], 71), 0)
    request_lengths = jax.vmap(lambda own: ragged_sizes(own, REQ_DEV, TOK_DEV, MOST_REQ, 2))(jax.random.split(key_of[1], SHARDS)).reshape((SHARDS, REQ_DEV)).astype(jnp.int32)
    w_qkv = draw_w_qkv(jax.random.fold_in(key_of[15], 71), 0)
    qk_gain = draw_qk_gain(jax.random.fold_in(key_of[15], 71), 0)
    w_out = centred(key_of[4], (D, D), D ** -0.5, 0.125, ((0, 2),))
    norm_gains = jnp.clip(1.0 + 0.15 * jax.random.normal(key_of[5], (3, D), jnp.float32), 0.25, 1.75)
    w_router = centred(key_of[6], (D, EXPERTS), (4 * D) ** -0.5, 0.0625)
    routes_keys = jax.random.split(jax.random.fold_in(key_of[7], 1), TOKENS // TOK_DEV)
    routes_turns = jax.random.permutation(jax.random.fold_in(key_of[7], 3), TOKENS // TOK_DEV)
    routes = jax.vmap(lambda own, number: deal_out(jax.random.fold_in(key_of[7], 2), own, number, TOK_DEV, EXPERTS, TOPK, CAP, 2))(routes_keys, routes_turns).reshape((TOKENS, TOPK))
    w_gate = centred(key_of[8], (EXPERTS, D, FF), D ** -0.5, 0.125, ((0, 16), (2, 2)))
    w_up = centred(key_of[9], (EXPERTS, D, FF), D ** -0.5, 0.125, ((0, 16), (2, 2)))
    w_down = centred(key_of[10], (EXPERTS, FF, D), FF ** -0.5, 0.1875, ((0, 16), (1, 2)))
    w_proj = centred(key_of[11], (D, EMB), D ** -0.5, 0.125)
    doc_vectors = centred(key_of[12], (HOLDERS * DOC_TOK, EMB), 1.0, 6.0, ((0, 32),))
    doc_segment = jax.vmap(lambda own: jnp.searchsorted(jnp.cumsum(ragged_sizes(own, DOCS_DEV, DOC_TOK, DOC_MOST, 2)), jnp.arange(DOC_TOK), side="right"))(jax.random.split(key_of[13], HOLDERS)).reshape((HOLDERS, DOC_TOK)).astype(jnp.int32)
    doc_request = touch_ends(jax.random.randint(key_of[14], (HOLDERS, DOCS_DEV), 0, REQUESTS), jax.random.fold_in(key_of[14], 1), 0, REQUESTS - 1).astype(jnp.int32)
    return {"tokens": tokens, "request_lengths": request_lengths, "w_qkv": w_qkv, "qk_gain": qk_gain, "w_out": w_out, "norm_gains": norm_gains, "w_router": w_router, "routes": routes, "w_gate": w_gate, "w_up": w_up, "w_down": w_down, "w_proj": w_proj, "doc_vectors": doc_vectors, "doc_segment": doc_segment, "doc_request": doc_request}


EPS = 1e-06
THETA = 50000.0
NEG = -1e+30

def rms_norm(values, gain):
    return values * lax.rsqrt(lax.optimization_barrier(jnp.mean(values * values, axis=-1, keepdims=True)) + EPS) * gain

def rotary(values, offsets):
    half = values.shape[-1] // 2
    freq = THETA ** (-jnp.arange(half, dtype=jnp.float32) / half)
    angle = offsets.astype(jnp.float32)[:, None] * freq[None, :]
    cosine = jnp.cos(angle)[:, None, :]
    sine = jnp.sin(angle)[:, None, :]
    first = values[..., :half]
    second = values[..., half:]
    return jnp.concatenate([first * cosine - second * sine, second * cosine + first * sine], axis=-1)

def request_layout(lengths_row, count):
    bounds = jnp.cumsum(lengths_row).astype(jnp.int32)
    places = jnp.arange(count, dtype=jnp.int32)
    member = lax.optimization_barrier(jnp.sum((places[:, None] >= bounds[None, :-1]).astype(jnp.int32), axis=1)).astype(jnp.int32)
    starts = (bounds - lengths_row).astype(jnp.int32)
    pick = member[:, None] == jnp.arange(lengths_row.shape[0], dtype=jnp.int32)[None, :]
    offsets = places - lax.optimization_barrier(jnp.sum(jnp.where(pick, starts[None, :], 0), axis=1)).astype(jnp.int32)
    return (member, offsets)

def reference(tokens, request_lengths, w_qkv, qk_gain, w_out, norm_gains, w_router, routes, w_gate, w_up, w_down, w_proj, doc_vectors, doc_segment, doc_request):
    f32 = jnp.float32
    bf16 = jnp.bfloat16
    scale = HD ** (-0.5)
    flat_qkv = w_qkv.reshape(D, 3 * D)
    expert_ids = jnp.arange(EXPERTS, dtype=jnp.int32)

    def front(item):
        x, lengths_row, route_rows = item
        member, offsets = request_layout(lengths_row, TOK_DEV)
        xf = x.astype(f32)
        normed = rms_norm(xf, norm_gains[0]).astype(bf16)
        proj = jnp.dot(normed, flat_qkv, preferred_element_type=f32).reshape(TOK_DEV, 3, HEADS, HD)
        query = rotary(rms_norm(proj[:, 0], qk_gain[0].reshape(HEADS, HD)), offsets).astype(bf16)
        keys = rotary(rms_norm(proj[:, 1], qk_gain[1].reshape(HEADS, HD)), offsets).astype(bf16)
        values = proj[:, 2].astype(bf16)
        scores = jnp.einsum('qhd,khd->hqk', query.astype(f32), keys.astype(f32)) * scale
        scores = jnp.where((member[:, None] == member[None, :])[None], scores, NEG)
        peak = lax.optimization_barrier(jnp.max(scores, axis=-1, keepdims=True))
        weights = jnp.exp(scores - peak)
        probs = (weights / lax.optimization_barrier(jnp.sum(weights, axis=-1, keepdims=True))).astype(bf16)
        mixed = jnp.einsum('hqk,khd->qhd', probs.astype(f32), values.astype(f32)).astype(bf16).reshape(TOK_DEV, D)
        attn = jnp.dot(mixed, w_out, preferred_element_type=f32)
        hidden = (xf + attn).astype(bf16)
        normed_two = rms_norm(hidden.astype(f32), norm_gains[1]).astype(bf16)
        logits = jnp.dot(normed_two, w_router, preferred_element_type=f32)
        onehot = route_rows[:, :, None] == expert_ids[None, None, :]
        chosen = lax.optimization_barrier(jnp.sum(jnp.where(onehot, logits[:, None, :], 0.0), axis=-1))
        lifted = jax.nn.sigmoid(chosen)
        gates = lifted / lax.optimization_barrier(jnp.sum(lifted, axis=-1, keepdims=True))
        counts = lax.optimization_barrier(jnp.sum(onehot.astype(f32), axis=1))
        before = jnp.cumsum(counts, axis=0) - counts
        slots = lax.optimization_barrier(jnp.sum(jnp.where(onehot, before[:, None, :], 0.0), axis=-1)).astype(jnp.int32)
        places = (route_rows * CAP + slots).astype(jnp.int32)
        owner = jnp.full((EXPERTS * CAP,), TOK_DEV, jnp.int32).at[places.reshape(-1)].set(jnp.repeat(jnp.arange(TOK_DEV, dtype=jnp.int32), TOPK))
        padded = jnp.concatenate([normed_two, jnp.zeros((1, D), bf16)], axis=0)
        buffer = padded[owner].reshape(EXPERTS, CAP, D)
        return (hidden, gates, slots, buffer)
    hiddens, gates, slots, buffers = lax.map(front, (tokens.reshape(SHARDS, TOK_DEV, D), request_lengths, routes.reshape(SHARDS, TOK_DEV, TOPK)))
    rows = buffers.transpose(1, 0, 2, 3).reshape(EXPERTS, SHARDS * CAP, D)
    narrow_ff = FF // N_NARROW

    def expert(item):
        block, wg, wu, wd = item
        gate = jnp.dot(block, wg, preferred_element_type=f32)
        upward = jnp.dot(block, wu, preferred_element_type=f32)
        act = (jax.nn.silu(gate) * upward).astype(bf16).reshape(SHARDS * CAP, N_NARROW, narrow_ff)
        parts = jnp.einsum('rnf,nfd->nrd', act.astype(f32), wd.reshape(N_NARROW, narrow_ff, D).astype(f32)).astype(bf16)
        parts = lax.optimization_barrier(parts)
        return lax.optimization_barrier(jnp.sum(parts.astype(f32), axis=0))
    outputs = lax.map(expert, (rows, w_gate, w_up, w_down)).reshape(EXPERTS * SHARDS * CAP, D)

    def back(item):
        hidden, gate_rows, slot_rows, route_rows, shard = item
        index = (route_rows * (SHARDS * CAP) + shard * CAP + slot_rows).astype(jnp.int32)
        picked = outputs[index]
        moe = lax.optimization_barrier(jnp.sum(gate_rows[:, :, None] * picked, axis=1))
        layer = (hidden.astype(f32) + moe).astype(bf16)
        normed_three = rms_norm(layer.astype(f32), norm_gains[2]).astype(bf16)
        embedded = jnp.dot(normed_three, w_proj, preferred_element_type=f32)
        vectors = (embedded * lax.rsqrt(lax.optimization_barrier(jnp.sum(embedded * embedded, axis=-1, keepdims=True)) + EPS)).astype(bf16)
        return (layer, vectors)
    layers, vectors = lax.map(back, (hiddens, gates, slots, routes.reshape(SHARDS, TOK_DEV, TOPK), jnp.arange(SHARDS, dtype=jnp.int32)))
    layer_out = layers.reshape(TOKENS, D)
    vectors = vectors.reshape(TOKENS, EMB)
    padded_q = jnp.concatenate([vectors, jnp.zeros((MOST_REQ, EMB), bf16)], axis=0)
    docs = jnp.concatenate([doc_vectors.reshape(HOLDERS, DOC_TOK, EMB), jnp.zeros((HOLDERS, DOC_MOST, EMB), bf16)], axis=1)
    bounds = jnp.cumsum(request_lengths, axis=1).astype(jnp.int32)
    starts = (bounds - request_lengths).astype(jnp.int32)
    flat_lengths = request_lengths.reshape(-1).astype(jnp.int32)
    flat_starts = (starts + jnp.arange(SHARDS, dtype=jnp.int32)[:, None] * TOK_DEV).reshape(-1).astype(jnp.int32)
    request_ids = jnp.arange(REQUESTS, dtype=jnp.int32)

    def holder_scores(item):
        held, segment_row, requests = item

        def one(doc, request):
            first = jnp.sum((segment_row < doc).astype(jnp.int32)).astype(jnp.int32)
            size = jnp.sum((segment_row == doc).astype(jnp.int32)).astype(jnp.int32)
            doc_rows = lax.dynamic_slice_in_dim(held, first, DOC_MOST, 0)
            pick = request == request_ids
            q_first = jnp.sum(jnp.where(pick, flat_starts, 0)).astype(jnp.int32)
            q_size = jnp.sum(jnp.where(pick, flat_lengths, 0)).astype(jnp.int32)
            queries = lax.dynamic_slice_in_dim(padded_q, q_first, MOST_REQ, 0)
            sims = jnp.dot(queries, doc_rows.T, preferred_element_type=f32)
            sims = jnp.where(jnp.arange(DOC_MOST, dtype=jnp.int32)[None, :] < size, sims, NEG)
            best = lax.optimization_barrier(jnp.max(sims, axis=1))
            used = jnp.arange(MOST_REQ, dtype=jnp.int32) < q_size
            return jnp.sum(jnp.where(used, best, 0.0)) / q_size.astype(f32)
        return jax.vmap(one)(jnp.arange(DOCS_DEV, dtype=jnp.int32), requests)
    doc_scores = lax.map(holder_scores, (docs, doc_segment, doc_request))
    return (layer_out, doc_scores)
```

```python
import functools

import jax
import jax.numpy as jnp
from jax import lax
from jax.experimental import pallas as pl
from jax.experimental.pallas import tpu as pltpu
from jax.sharding import PartitionSpec as P

HD = 128
TOK_DEV = 128
MOST_REQ = 64
DOC_MOST = 128
LANES = 128

EPS = 1e-06
THETA = 50000.0
NEG = -1e30
MIB = 1 << 20

f32 = jnp.float32
bf16 = jnp.bfloat16
VMEM = pl.BlockSpec(memory_space=pltpu.VMEM)


def rms_norm(values, gain):
    return values * lax.rsqrt(jnp.mean(values * values, axis=-1, keepdims=True) + EPS) * gain


def request_layout(lengths_row, count):
    bounds = jnp.cumsum(lengths_row)
    places = jnp.arange(count, dtype=jnp.int32)
    member = jnp.sum((places[:, None] >= bounds[None, :-1]).astype(jnp.int32), axis=1)
    starts = bounds - lengths_row
    pick = member[:, None] == jnp.arange(lengths_row.shape[0], dtype=jnp.int32)[None, :]
    offsets = places - jnp.sum(jnp.where(pick, starts[None, :], 0), axis=1)
    return (member, offsets)


def front_kernel(tokens, gain, w_qkv, qk_gain, cosine, sine, bias, mixed, normed):
    @pl.when(pl.program_id(0) == 0)
    def _():
        normed[...] = rms_norm(tokens[...].astype(f32), gain[...]).astype(bf16)

    heads = mixed.shape[1] // HD
    parts = [jnp.dot(normed[...], w_qkv[i], preferred_element_type=f32) for i in range(3)]
    for head in range(heads):
        lanes = slice(head * HD, (head + 1) * HD)

        def turned(part):
            v = rms_norm(parts[part][:, lanes], qk_gain[part : part + 1, lanes])
            return (v * cosine[...] + pltpu.roll(v, HD // 2, 1) * sine[...]).astype(bf16)

        query, keys = turned(0), turned(1)
        values = parts[2][:, lanes].astype(bf16)
        scores = lax.dot_general(
            query, keys, (((1,), (1,)), ((), ())), preferred_element_type=f32
        ) * (HD ** (-0.5))
        scores = jnp.where(bias[...] > 0, scores, NEG)
        weights = jnp.exp(scores - jnp.max(scores, axis=-1, keepdims=True))
        probs = (weights / jnp.sum(weights, axis=-1, keepdims=True)).astype(bf16)
        mixed[:, lanes] = jnp.dot(probs, values, preferred_element_type=f32).astype(bf16)


def partner_barrier(other):
    barrier = pltpu.get_barrier_semaphore()
    pl.semaphore_signal(
        barrier, inc=1, device_id={"narrow": other}, device_id_type=pl.DeviceIdType.MESH
    )
    pl.semaphore_wait(barrier, 1)


def join_kernel(
    pieces, experts, mixed, w_out, tokens, gain, w_router, routes,
    hidden, extended, mine, theirs, send_sem, recv_sem,
):
    other = 1 - lax.axis_index("narrow")
    partner_barrier(other)
    width = w_out.shape[1]
    step = width // pieces
    copies = []
    for piece in range(pieces):
        lanes = pl.ds(piece * step, step)
        mine[piece] = jnp.dot(mixed[...], w_out[:, lanes], preferred_element_type=f32).astype(bf16)
        copy = pltpu.make_async_remote_copy(
            src_ref=mine.at[piece],
            dst_ref=theirs.at[piece],
            send_sem=send_sem.at[piece],
            recv_sem=recv_sem.at[piece],
            device_id={"narrow": other},
            device_id_type=pl.DeviceIdType.MESH,
        )
        copy.start()
        copies.append(copy)
    total = 0.0
    for piece in range(pieces):
        lanes = pl.ds(piece * step, step)
        copies[piece].wait()
        attn = mine[piece].astype(f32) + theirs[piece].astype(f32)
        row = (tokens[:, lanes].astype(f32) + attn).astype(bf16)
        hidden[:, lanes] = row
        row = row.astype(f32)
        total = total + jnp.sum(row * row, axis=-1, keepdims=True)
    scale = lax.rsqrt(total / width + EPS)
    normed = (hidden[...].astype(f32) * scale * gain[...]).astype(bf16)
    extended[:, :width] = normed
    logits = jnp.dot(normed, w_router[...], preferred_element_type=f32)
    lane = lax.broadcasted_iota(jnp.int32, logits.shape, 1)
    expert = jnp.where(lane < experts, lane, lane - experts)
    routed = routes[:, 0:1] == expert
    for k in range(1, routes.shape[1]):
        routed = routed | (routes[:, k : k + 1] == expert)
    lifted = jnp.where(routed, 1.0 / (1.0 + jnp.exp(-logits)), 0.0)
    first = lane < experts
    gates = lifted / jnp.sum(jnp.where(first, lifted, 0.0), axis=-1, keepdims=True)
    high = gates.astype(bf16).astype(f32)
    extended[:, width:] = jnp.where(first, high, gates - high).astype(bf16)


def moe_kernel(rows, chosen, w_gate, w_up, w_down, out):
    width = out.shape[1]
    x = rows[:, :width]
    table = rows[:, width:].astype(f32)
    total = 0.0
    for e in range(w_gate.shape[0]):
        gate = jnp.sum(table * chosen[e : e + 1, :], axis=-1, keepdims=True)
        lift = jnp.dot(x, w_gate[e], preferred_element_type=f32)
        upward = jnp.dot(x, w_up[e], preferred_element_type=f32)
        active = (lift / (1.0 + jnp.exp(-lift)) * upward * gate).astype(bf16)
        total = total + jnp.dot(active, w_down[e], preferred_element_type=f32)
    out[...] = total.astype(bf16)


def tail_kernel(
    pieces, partial_out, hidden, gain, w_proj, layer_out, vectors, theirs, send_sem, recv_sem
):
    other = 1 - lax.axis_index("narrow")
    partner_barrier(other)
    width = hidden.shape[1]
    step = hidden.shape[0] // pieces
    copies = []
    for piece in range(pieces):
        rows = pl.ds(piece * step, step)
        copy = pltpu.make_async_remote_copy(
            src_ref=partial_out.at[rows],
            dst_ref=theirs.at[rows],
            send_sem=send_sem.at[piece],
            recv_sem=recv_sem.at[piece],
            device_id={"narrow": other},
            device_id_type=pl.DeviceIdType.MESH,
        )
        copy.start()
        copies.append(copy)
    for piece in range(pieces):
        rows = pl.ds(piece * step, step)
        copies[piece].wait()
        moe = partial_out[rows, :].astype(f32) + theirs[rows, :].astype(f32)
        out = (hidden[rows, :].astype(f32) + moe).astype(bf16)
        layer_out[rows, :] = out
        normed = rms_norm(out.astype(f32), gain[...]).astype(bf16)
        embedded = jnp.dot(normed, w_proj[...], preferred_element_type=f32)
        vectors[rows, :] = (
            embedded * lax.rsqrt(jnp.sum(embedded * embedded, axis=-1, keepdims=True) + EPS)
        ).astype(bf16)


def docs_kernel(plan, vectors, docs, scores):
    held = scores.shape[1]
    q_rows = MOST_REQ + 16
    d_rows = DOC_MOST + 128
    lane = lax.broadcasted_iota(jnp.int32, (1, held), 1)
    row = lax.broadcasted_iota(jnp.int32, (q_rows, 1), 0)
    column = lax.broadcasted_iota(jnp.int32, (1, d_rows), 1)
    out = jnp.zeros((1, held), f32)
    for doc in range(held):
        q_first, q_size = plan[0, doc], plan[1, doc]
        d_first, d_size = plan[2, doc], plan[3, doc]
        q_at = pl.multiple_of(jnp.minimum(q_first // 16 * 16, vectors.shape[0] - q_rows), 16)
        d_at = pl.multiple_of(jnp.minimum(d_first // 16 * 16, docs.shape[0] - d_rows), 16)
        sims = lax.dot_general(
            vectors[pl.ds(q_at, q_rows), :],
            docs[pl.ds(d_at, d_rows), :],
            (((1,), (1,)), ((), ())),
            preferred_element_type=f32,
        )
        place = column + d_at
        sims = jnp.where((place >= d_first) & (place < d_first + d_size), sims, NEG)
        best = jnp.max(sims, axis=1, keepdims=True)
        place = row + q_at
        best = jnp.where((place >= q_first) & (place < q_first + q_size), best, 0.0)
        total = jnp.sum(best, axis=0, keepdims=True) / q_size.astype(f32)
        out = jnp.where(lane == doc, total, out)
    scores[...] = out


def body(
    tokens,
    request_lengths,
    w_qkv,
    qk_gain,
    w_out,
    norm_gains,
    w_router,
    routes,
    w_gate,
    w_up,
    w_down,
    w_proj,
    doc_vectors,
    doc_segment,
    doc_request,
):
    count, width = tokens.shape
    experts = w_router.shape[1]
    experts_here = w_gate.shape[0]
    columns = w_qkv.shape[2]
    shards = request_lengths.shape[0]
    wide = lax.axis_index("wide")
    narrow = lax.axis_index("narrow")

    lengths_row = lax.dynamic_slice_in_dim(request_lengths, wide, 1, 0)[0]
    member, offsets = request_layout(lengths_row, count)
    half = HD // 2
    freq = THETA ** (-jnp.arange(half, dtype=f32) / half)
    angle = offsets.astype(f32)[:, None] * freq[None, :]
    cosine, sine = jnp.cos(angle), jnp.sin(angle)
    cosine = jnp.concatenate([cosine, cosine], axis=1)
    sine = jnp.concatenate([-sine, sine], axis=1)
    same = (member[:, None] == member[None, :]).astype(f32)

    block = 256
    mixed = pl.pallas_call(
        front_kernel,
        out_shape=jax.ShapeDtypeStruct((count, columns), bf16),
        grid=(columns // block,),
        in_specs=[
            pl.BlockSpec((count, width), lambda i: (0, 0)),
            pl.BlockSpec((1, width), lambda i: (0, 0)),
            pl.BlockSpec((3, width, block), lambda i: (0, 0, i)),
            pl.BlockSpec((2, block), lambda i: (0, i)),
            pl.BlockSpec((count, HD), lambda i: (0, 0)),
            pl.BlockSpec((count, HD), lambda i: (0, 0)),
            pl.BlockSpec((count, count), lambda i: (0, 0)),
        ],
        out_specs=pl.BlockSpec((count, block), lambda i: (0, i)),
        scratch_shapes=[pltpu.VMEM((count, width), bf16)],
        compiler_params=pltpu.CompilerParams(vmem_limit_bytes=24 * MIB),
        name="front",
    )(tokens, norm_gains[0:1], jnp.transpose(w_qkv, (1, 0, 2)), qk_gain, cosine, sine, same)

    extra = (2 * experts + LANES - 1) // LANES * LANES
    routers = jnp.concatenate(
        [w_router, w_router, jnp.zeros((width, extra - 2 * experts), bf16)], axis=1
    )
    pieces = 4
    hidden, extended = pl.pallas_call(
        functools.partial(join_kernel, pieces, experts),
        out_shape=(
            jax.ShapeDtypeStruct((count, width), bf16),
            jax.ShapeDtypeStruct((count, width + extra), bf16),
        ),
        in_specs=[VMEM] * 6,
        out_specs=(VMEM, VMEM),
        scratch_shapes=[
            pltpu.VMEM((pieces, count, width // pieces), bf16),
            pltpu.VMEM((pieces, count, width // pieces), bf16),
            pltpu.SemaphoreType.DMA((pieces,)),
            pltpu.SemaphoreType.DMA((pieces,)),
        ],
        compiler_params=pltpu.CompilerParams(
            collective_id=0, has_side_effects=True, vmem_limit_bytes=24 * MIB
        ),
        name="join",
    )(mixed, w_out, tokens, norm_gains[1:2], routers, routes)

    share = count // lax.axis_size("narrow")
    own_rows = lax.dynamic_slice_in_dim(extended, narrow * share, share, 0)
    rows = lax.all_gather(own_rows, ("wide", "narrow"), axis=0, tiled=True)

    ids = wide * experts_here + jnp.arange(experts_here, dtype=jnp.int32)
    lane = jnp.arange(extra, dtype=jnp.int32)[None, :]
    chosen = ((lane == ids[:, None]) | (lane == ids[:, None] + experts)).astype(f32)
    every = rows.shape[0]
    block = 256
    partial_out = pl.pallas_call(
        moe_kernel,
        out_shape=jax.ShapeDtypeStruct((every, width), bf16),
        grid=(every // block,),
        in_specs=[
            pl.BlockSpec((block, width + extra), lambda i: (i, 0)),
            pl.BlockSpec(chosen.shape, lambda i: (0, 0)),
            pl.BlockSpec(w_gate.shape, lambda i: (0, 0, 0)),
            pl.BlockSpec(w_up.shape, lambda i: (0, 0, 0)),
            pl.BlockSpec(w_down.shape, lambda i: (0, 0, 0)),
        ],
        out_specs=pl.BlockSpec((block, width), lambda i: (i, 0)),
        compiler_params=pltpu.CompilerParams(vmem_limit_bytes=48 * MIB),
        name="experts",
    )(rows, chosen, w_gate, w_up, w_down)

    scattered = lax.psum_scatter(partial_out, "wide", scatter_dimension=0, tiled=True)

    pieces = 4
    layer_out, vectors = pl.pallas_call(
        functools.partial(tail_kernel, pieces),
        out_shape=(
            jax.ShapeDtypeStruct((count, width), bf16),
            jax.ShapeDtypeStruct((count, w_proj.shape[1]), bf16),
        ),
        in_specs=[VMEM] * 4,
        out_specs=(VMEM, VMEM),
        scratch_shapes=[
            pltpu.VMEM((count, width), bf16),
            pltpu.SemaphoreType.DMA((pieces,)),
            pltpu.SemaphoreType.DMA((pieces,)),
        ],
        compiler_params=pltpu.CompilerParams(
            collective_id=1, has_side_effects=True, vmem_limit_bytes=24 * MIB
        ),
        name="tail",
    )(scattered, hidden, norm_gains[2:3], w_proj)

    every_vector = lax.all_gather(vectors, "wide", axis=0, tiled=True)

    flat_lengths = request_lengths.reshape(-1)
    starts = jnp.cumsum(request_lengths, axis=1) - request_lengths
    flat_starts = (starts + TOK_DEV * jnp.arange(shards, dtype=jnp.int32)[:, None]).reshape(-1)
    requests = doc_request[0]
    pick = requests[:, None] == jnp.arange(flat_lengths.shape[0], dtype=jnp.int32)[None, :]
    docs = jnp.arange(requests.shape[0], dtype=jnp.int32)[:, None]
    plan = jnp.stack(
        [
            jnp.sum(jnp.where(pick, flat_starts[None, :], 0), axis=1),
            jnp.sum(jnp.where(pick, flat_lengths[None, :], 0), axis=1),
            jnp.sum((doc_segment < docs).astype(jnp.int32), axis=1),
            jnp.sum((doc_segment == docs).astype(jnp.int32), axis=1),
        ]
    )
    doc_scores = pl.pallas_call(
        docs_kernel,
        out_shape=jax.ShapeDtypeStruct((1, requests.shape[0]), f32),
        in_specs=[pl.BlockSpec(memory_space=pltpu.SMEM), VMEM, VMEM],
        out_specs=VMEM,
        name="docs",
    )(plan, every_vector, doc_vectors)
    return (layer_out, doc_scores)


def solution(mesh):
    placed = (
        P("wide", None),
        P(),
        P(None, None, "narrow"),
        P(None, "narrow"),
        P("narrow", None),
        P(),
        P(),
        P("wide", None),
        P("wide", None, "narrow"),
        P("wide", None, "narrow"),
        P("wide", "narrow", None),
        P(),
        P(("wide", "narrow"), None),
        P(("wide", "narrow"), None),
        P(("wide", "narrow"), None),
    )
    return jax.shard_map(
        body,
        mesh=mesh,
        in_specs=placed,
        out_specs=(P("wide", None), P(("wide", "narrow"), None)),
        check_vma=False,
    )
```

```python
import functools

import jax
import jax.numpy as jnp
from jax import lax
from jax.experimental import pallas as pl
from jax.experimental.pallas import tpu as pltpu
from jax.sharding import PartitionSpec as P

HD = 128
TOK_DEV = 128
MOST_REQ = 64
DOC_MOST = 128
LANES = 128

EPS = 1e-06
THETA = 50000.0
NEG = -1e30
MIB = 1 << 20

f32 = jnp.float32
bf16 = jnp.bfloat16
VMEM = pl.BlockSpec(memory_space=pltpu.VMEM)


def rms_norm(values, gain):
    return values * lax.rsqrt(jnp.mean(values * values, axis=-1, keepdims=True) + EPS) * gain


def request_layout(lengths_row, count):
    bounds = jnp.cumsum(lengths_row)
    places = jnp.arange(count, dtype=jnp.int32)
    member = jnp.sum((places[:, None] >= bounds[None, :-1]).astype(jnp.int32), axis=1)
    starts = bounds - lengths_row
    pick = member[:, None] == jnp.arange(lengths_row.shape[0], dtype=jnp.int32)[None, :]
    offsets = places - jnp.sum(jnp.where(pick, starts[None, :], 0), axis=1)
    return (member, offsets)


def front_kernel(tokens, gain, w_qkv, qk_gain, cosine, sine, bias, mixed, normed):
    @pl.when(pl.program_id(0) == 0)
    def _():
        normed[...] = rms_norm(tokens[...].astype(f32), gain[...]).astype(bf16)

    heads = mixed.shape[1] // HD
    parts = [jnp.dot(normed[...], w_qkv[i], preferred_element_type=f32) for i in range(3)]
    for head in range(heads):
        lanes = slice(head * HD, (head + 1) * HD)

        def turned(part):
            v = rms_norm(parts[part][:, lanes], qk_gain[part : part + 1, lanes])
            return (v * cosine[...] + pltpu.roll(v, HD // 2, 1) * sine[...]).astype(bf16)

        query, keys = turned(0), turned(1)
        values = parts[2][:, lanes].astype(bf16)
        scores = lax.dot_general(
            query, keys, (((1,), (1,)), ((), ())), preferred_element_type=f32
        ) * (HD ** (-0.5))
        scores = jnp.where(bias[...] > 0, scores, NEG)
        weights = jnp.exp(scores - jnp.max(scores, axis=-1, keepdims=True))
        probs = (weights / jnp.sum(weights, axis=-1, keepdims=True)).astype(bf16)
        mixed[:, lanes] = jnp.dot(probs, values, preferred_element_type=f32).astype(bf16)


def partner_barrier(peers):
    barrier = pltpu.get_barrier_semaphore()
    me = lax.axis_index("narrow")
    for k in range(1, peers):
        pl.semaphore_signal(
            barrier,
            inc=1,
            device_id={"narrow": (me + k) % peers},
            device_id_type=pl.DeviceIdType.MESH,
        )
    pl.semaphore_wait(barrier, peers - 1)


def send_peers(peers, src, slot, send_sem, recv_sem, piece):
    me = lax.axis_index("narrow")
    copies = []
    for k in range(1, peers):
        copy = pltpu.make_async_remote_copy(
            src_ref=src,
            dst_ref=slot(k),
            send_sem=send_sem.at[k, piece],
            recv_sem=recv_sem.at[k, piece],
            device_id={"narrow": (me + k) % peers},
            device_id_type=pl.DeviceIdType.MESH,
        )
        copy.start()
        copies.append(copy)
    return copies


def sum_peers(peers, load):
    me = lax.axis_index("narrow")
    return sum(load((me - j + peers) % peers).astype(f32) for j in range(peers))


def join_kernel(
    peers, pieces, experts, mixed, w_out, tokens, gain, w_router, routes,
    hidden, extended, parts, send_sem, recv_sem,
):
    partner_barrier(peers)
    width = w_out.shape[1]
    step = width // pieces
    copies = []
    for piece in range(pieces):
        lanes = pl.ds(piece * step, step)
        parts[0, piece] = jnp.dot(
            mixed[...], w_out[:, lanes], preferred_element_type=f32
        ).astype(bf16)
        copies.append(
            send_peers(
                peers,
                parts.at[0, piece],
                lambda k: parts.at[k, piece],
                send_sem,
                recv_sem,
                piece,
            )
        )
    total = 0.0
    for piece in range(pieces):
        lanes = pl.ds(piece * step, step)
        for copy in copies[piece]:
            copy.wait()
        attn = sum_peers(peers, lambda k: parts[k, piece])
        row = (tokens[:, lanes].astype(f32) + attn).astype(bf16)
        hidden[:, lanes] = row
        row = row.astype(f32)
        total = total + jnp.sum(row * row, axis=-1, keepdims=True)
    scale = lax.rsqrt(total / width + EPS)
    normed = (hidden[...].astype(f32) * scale * gain[...]).astype(bf16)
    extended[:, :width] = normed
    logits = jnp.dot(normed, w_router[...], preferred_element_type=f32)
    lane = lax.broadcasted_iota(jnp.int32, logits.shape, 1)
    expert = jnp.where(lane < experts, lane, lane - experts)
    routed = routes[:, 0:1] == expert
    for k in range(1, routes.shape[1]):
        routed = routed | (routes[:, k : k + 1] == expert)
    lifted = jnp.where(routed, 1.0 / (1.0 + jnp.exp(-logits)), 0.0)
    first = lane < experts
    gates = lifted / jnp.sum(jnp.where(first, lifted, 0.0), axis=-1, keepdims=True)
    high = gates.astype(bf16).astype(f32)
    extended[:, width:] = jnp.where(first, high, gates - high).astype(bf16)


def gather_kernel(depth, own, out, local_sem, z_sem, x_sem, y_sem, dx_sem, dy_sem, core_sem):
    wide, narrow = lax.axis_index("wide"), lax.axis_index("narrow")
    z, side, core = wide // 4, wide // 2 % 2, wide % 2
    share = own.shape[0]
    half = share // 2
    to_up, to_down = {"wide": wide + 4}, {"wide": wide - 4}
    to_x, to_y = {"wide": wide + 2 - 4 * side}, {"narrow": 1 - narrow}
    to_core = {"wide": wide + 1 - 2 * core}

    barrier = pltpu.get_barrier_semaphore()

    def greet(device):
        pl.semaphore_signal(
            barrier, inc=1, device_id=device, device_id_type=pl.DeviceIdType.MESH
        )

    for device in (to_x, to_y, to_core):
        greet(device)
    pl.when(z < depth - 1)(lambda: greet(to_up))
    pl.when(z > 0)(lambda: greet(to_down))
    pl.semaphore_wait(barrier, 3 + (z + depth - 1) // depth + (2 * depth - 2 - z) // depth)

    def place(s, across_x, across_y, part=None, cores=core):
        along = 1 - side if across_x else side
        lane = 1 - narrow if across_y else narrow
        at = ((s * 4 + along * 2 + cores) * 2 + lane) * share
        if part is None:
            return out.at[pl.ds(pl.multiple_of(at, 16), share)]
        return out.at[pl.ds(pl.multiple_of(at + part * half, 16), half)]

    def copy(ref, sems, index, device):
        return pltpu.make_async_remote_copy(
            src_ref=ref,
            dst_ref=ref,
            send_sem=sems.at[0, index],
            recv_sem=sems.at[1, index],
            device_id=device,
            device_id_type=pl.DeviceIdType.MESH,
        )

    def upward(s):
        return copy(place(s, 0, 0), z_sem, s, to_up)

    def downward(s):
        return copy(place(s, 0, 0), z_sem, s + depth, to_down)

    def cross(s, kind):
        return copy(place(s, kind & 1, kind >> 1), core_sem, s * 4 + kind, to_core)

    def over_x(s):
        return copy(place(s, 0, 0), x_sem, s, to_x)

    def over_y(s):
        return copy(place(s, 0, 0), y_sem, s, to_y)

    def corner_y(s):
        return copy(place(s, 1, 0, 0), dy_sem, s, to_y)

    def corner_x(s):
        return copy(place(s, 0, 1, 1), dx_sem, s, to_x)

    def first(s, up, down):
        if up:
            pl.when(z < depth - 1)(lambda: upward(s).start())
        if down:
            pl.when(z > 0)(lambda: downward(s).start())
        over_x(s).start()
        over_y(s).start()
        cross(s, 0).start()

    def second(s):
        over_x(s).wait_recv()
        corner_y(s).start()
        cross(s, 1).start()
        over_y(s).wait_recv()
        corner_x(s).start()
        cross(s, 2).start()

    def third(s):
        corner_y(s).wait_recv()
        corner_x(s).wait_recv()
        cross(s, 3).start()

    def at_distance(d, do):
        if d == 0:
            do(z, True, True)
            return
        pl.when(z >= d)(lambda: do(z - d, True, False))
        pl.when(z + d < depth)(lambda: do(z + d, False, True))

    def begin(s, up, down):
        if not (up and down):
            (upward(s) if up else downward(s)).wait_recv()
        first(s, up, down)

    keep = pltpu.make_async_copy(own, place(z, 0, 0), local_sem)
    keep.start()
    keep.wait()
    for d in range(depth + 2):
        if d < depth:
            at_distance(d, begin)
        if 0 <= d - 1 < depth:
            at_distance(d - 1, lambda s, up, down: second(s))
        if 0 <= d - 2:
            at_distance(d - 2, lambda s, up, down: third(s))

    def finish(s, up, down):
        if up:
            pl.when(z < depth - 1)(lambda: upward(s).wait_send())
        if down:
            pl.when(z > 0)(lambda: downward(s).wait_send())
        for done in (over_x(s), over_y(s), corner_x(s), corner_y(s)):
            done.wait_send()
        for kind in range(4):
            cross(s, kind).wait()

    for d in range(depth):
        at_distance(d, finish)


def gather(own, identity, name):
    if lax.axis_size("narrow") != 2 or lax.axis_size("wide") % 4:
        return lax.all_gather(own, ("wide", "narrow"), axis=0, tiled=True)
    devices = lax.axis_size("wide") * lax.axis_size("narrow")
    depth = lax.axis_size("wide") // 4
    pair = pltpu.SemaphoreType.DMA((2, depth))
    return pl.pallas_call(
        functools.partial(gather_kernel, depth),
        out_shape=jax.ShapeDtypeStruct((devices * own.shape[0], own.shape[1]), own.dtype),
        in_specs=[pl.BlockSpec(memory_space=pl.ANY)],
        out_specs=pl.BlockSpec(memory_space=pl.ANY),
        scratch_shapes=[
            pltpu.SemaphoreType.DMA,
            pltpu.SemaphoreType.DMA((2, 2 * depth)),
            pair,
            pair,
            pair,
            pair,
            pltpu.SemaphoreType.DMA((2, 4 * depth)),
        ],
        compiler_params=pltpu.CompilerParams(collective_id=identity, has_side_effects=True),
        name=name,
    )(own)


def moe_kernel(rows, chosen, w_gate, w_up, w_down, out):
    width = out.shape[1]
    x = rows[:, :width]
    table = rows[:, width:].astype(f32)
    total = 0.0
    for e in range(w_gate.shape[0]):
        gate = jnp.sum(table * chosen[e : e + 1, :], axis=-1, keepdims=True)
        lift = jnp.dot(x, w_gate[e], preferred_element_type=f32)
        upward = jnp.dot(x, w_up[e], preferred_element_type=f32)
        active = (lift / (1.0 + jnp.exp(-lift)) * upward * gate).astype(bf16)
        total = total + jnp.dot(active, w_down[e], preferred_element_type=f32)
    out[...] = total.astype(bf16)


def tail_kernel(
    peers, pieces, partial_out, hidden, gain, w_proj,
    layer_out, vectors, theirs, send_sem, recv_sem,
):
    partner_barrier(peers)
    step = hidden.shape[0] // pieces
    copies = []
    for piece in range(pieces):
        rows = pl.ds(piece * step, step)
        copies.append(
            send_peers(
                peers,
                partial_out.at[rows],
                lambda k: theirs.at[k, rows],
                send_sem,
                recv_sem,
                piece,
            )
        )
    theirs[0] = partial_out[...]
    for piece in range(pieces):
        rows = pl.ds(piece * step, step)
        for copy in copies[piece]:
            copy.wait()
        moe = sum_peers(peers, lambda k: theirs[k, rows, :])
        out = (hidden[rows, :].astype(f32) + moe).astype(bf16)
        layer_out[rows, :] = out
        normed = rms_norm(out.astype(f32), gain[...]).astype(bf16)
        embedded = jnp.dot(normed, w_proj[...], preferred_element_type=f32)
        vectors[rows, :] = (
            embedded * lax.rsqrt(jnp.sum(embedded * embedded, axis=-1, keepdims=True) + EPS)
        ).astype(bf16)


def docs_kernel(plan, vectors, docs, scores):
    held = scores.shape[1]
    q_rows = MOST_REQ + 16
    d_rows = DOC_MOST + 128
    lane = lax.broadcasted_iota(jnp.int32, (1, held), 1)
    row = lax.broadcasted_iota(jnp.int32, (q_rows, 1), 0)
    column = lax.broadcasted_iota(jnp.int32, (1, d_rows), 1)
    out = jnp.zeros((1, held), f32)
    for doc in range(held):
        q_first, q_size = plan[0, doc], plan[1, doc]
        d_first, d_size = plan[2, doc], plan[3, doc]
        q_at = pl.multiple_of(jnp.minimum(q_first // 16 * 16, vectors.shape[0] - q_rows), 16)
        d_at = pl.multiple_of(jnp.minimum(d_first // 16 * 16, docs.shape[0] - d_rows), 16)
        sims = lax.dot_general(
            vectors[pl.ds(q_at, q_rows), :],
            docs[pl.ds(d_at, d_rows), :],
            (((1,), (1,)), ((), ())),
            preferred_element_type=f32,
        )
        place = column + d_at
        sims = jnp.where((place >= d_first) & (place < d_first + d_size), sims, NEG)
        best = jnp.max(sims, axis=1, keepdims=True)
        place = row + q_at
        best = jnp.where((place >= q_first) & (place < q_first + q_size), best, 0.0)
        total = jnp.sum(best, axis=0, keepdims=True) / q_size.astype(f32)
        out = jnp.where(lane == doc, total, out)
    scores[...] = out


def body(
    tokens,
    request_lengths,
    w_qkv,
    qk_gain,
    w_out,
    norm_gains,
    w_router,
    routes,
    w_gate,
    w_up,
    w_down,
    w_proj,
    doc_vectors,
    doc_segment,
    doc_request,
):
    count, width = tokens.shape
    experts = w_router.shape[1]
    experts_here = w_gate.shape[0]
    columns = w_qkv.shape[2]
    shards = request_lengths.shape[0]
    wide = lax.axis_index("wide")
    narrow = lax.axis_index("narrow")
    peers = lax.axis_size("narrow")

    lengths_row = lax.dynamic_slice_in_dim(request_lengths, wide, 1, 0)[0]
    member, offsets = request_layout(lengths_row, count)
    half = HD // 2
    freq = THETA ** (-jnp.arange(half, dtype=f32) / half)
    angle = offsets.astype(f32)[:, None] * freq[None, :]
    cosine, sine = jnp.cos(angle), jnp.sin(angle)
    cosine = jnp.concatenate([cosine, cosine], axis=1)
    sine = jnp.concatenate([-sine, sine], axis=1)
    same = (member[:, None] == member[None, :]).astype(f32)

    block = 256
    mixed = pl.pallas_call(
        front_kernel,
        out_shape=jax.ShapeDtypeStruct((count, columns), bf16),
        grid=(columns // block,),
        in_specs=[
            pl.BlockSpec((count, width), lambda i: (0, 0)),
            pl.BlockSpec((1, width), lambda i: (0, 0)),
            pl.BlockSpec((3, width, block), lambda i: (0, 0, i)),
            pl.BlockSpec((2, block), lambda i: (0, i)),
            pl.BlockSpec((count, HD), lambda i: (0, 0)),
            pl.BlockSpec((count, HD), lambda i: (0, 0)),
            pl.BlockSpec((count, count), lambda i: (0, 0)),
        ],
        out_specs=pl.BlockSpec((count, block), lambda i: (0, i)),
        scratch_shapes=[pltpu.VMEM((count, width), bf16)],
        compiler_params=pltpu.CompilerParams(vmem_limit_bytes=24 * MIB),
        name="front",
    )(tokens, norm_gains[0:1], jnp.transpose(w_qkv, (1, 0, 2)), qk_gain, cosine, sine, same)

    extra = (2 * experts + LANES - 1) // LANES * LANES
    routers = jnp.concatenate(
        [w_router, w_router, jnp.zeros((width, extra - 2 * experts), bf16)], axis=1
    )
    pieces = 4
    hidden, extended = pl.pallas_call(
        functools.partial(join_kernel, peers, pieces, experts),
        out_shape=(
            jax.ShapeDtypeStruct((count, width), bf16),
            jax.ShapeDtypeStruct((count, width + extra), bf16),
        ),
        in_specs=[VMEM] * 6,
        out_specs=(VMEM, VMEM),
        scratch_shapes=[
            pltpu.VMEM((peers, pieces, count, width // pieces), bf16),
            pltpu.SemaphoreType.DMA((peers, pieces)),
            pltpu.SemaphoreType.DMA((peers, pieces)),
        ],
        compiler_params=pltpu.CompilerParams(
            collective_id=0, has_side_effects=True, vmem_limit_bytes=24 * MIB
        ),
        name="join",
    )(mixed, w_out, tokens, norm_gains[1:2], routers, routes)

    share = count // peers
    own_rows = lax.dynamic_slice_in_dim(extended, narrow * share, share, 0)
    rows = gather(own_rows, 2, "gather_rows")

    ids = wide * experts_here + jnp.arange(experts_here, dtype=jnp.int32)
    lane = jnp.arange(extra, dtype=jnp.int32)[None, :]
    chosen = ((lane == ids[:, None]) | (lane == ids[:, None] + experts)).astype(f32)
    every = rows.shape[0]
    block = 256
    partial_out = pl.pallas_call(
        moe_kernel,
        out_shape=jax.ShapeDtypeStruct((every, width), bf16),
        grid=(every // block,),
        in_specs=[
            pl.BlockSpec((block, width + extra), lambda i: (i, 0)),
            pl.BlockSpec(chosen.shape, lambda i: (0, 0)),
            pl.BlockSpec(w_gate.shape, lambda i: (0, 0, 0)),
            pl.BlockSpec(w_up.shape, lambda i: (0, 0, 0)),
            pl.BlockSpec(w_down.shape, lambda i: (0, 0, 0)),
        ],
        out_specs=pl.BlockSpec((block, width), lambda i: (i, 0)),
        compiler_params=pltpu.CompilerParams(vmem_limit_bytes=48 * MIB),
        name="experts",
    )(rows, chosen, w_gate, w_up, w_down)

    scattered = lax.psum_scatter(partial_out, "wide", scatter_dimension=0, tiled=True)

    pieces = 4
    layer_out, vectors = pl.pallas_call(
        functools.partial(tail_kernel, peers, pieces),
        out_shape=(
            jax.ShapeDtypeStruct((count, width), bf16),
            jax.ShapeDtypeStruct((count, w_proj.shape[1]), bf16),
        ),
        in_specs=[VMEM] * 4,
        out_specs=(VMEM, VMEM),
        scratch_shapes=[
            pltpu.VMEM((peers, count, width), bf16),
            pltpu.SemaphoreType.DMA((peers, pieces)),
            pltpu.SemaphoreType.DMA((peers, pieces)),
        ],
        compiler_params=pltpu.CompilerParams(
            collective_id=1, has_side_effects=True, vmem_limit_bytes=24 * MIB
        ),
        name="tail",
    )(scattered, hidden, norm_gains[2:3], w_proj)

    own_vectors = lax.dynamic_slice_in_dim(vectors, narrow * share, share, 0)
    every_vector = gather(own_vectors, 3, "gather_vectors")

    flat_lengths = request_lengths.reshape(-1)
    starts = jnp.cumsum(request_lengths, axis=1) - request_lengths
    flat_starts = (starts + TOK_DEV * jnp.arange(shards, dtype=jnp.int32)[:, None]).reshape(-1)
    requests = doc_request[0]
    pick = requests[:, None] == jnp.arange(flat_lengths.shape[0], dtype=jnp.int32)[None, :]
    docs = jnp.arange(requests.shape[0], dtype=jnp.int32)[:, None]
    plan = jnp.stack(
        [
            jnp.sum(jnp.where(pick, flat_starts[None, :], 0), axis=1),
            jnp.sum(jnp.where(pick, flat_lengths[None, :], 0), axis=1),
            jnp.sum((doc_segment < docs).astype(jnp.int32), axis=1),
            jnp.sum((doc_segment == docs).astype(jnp.int32), axis=1),
        ]
    )
    doc_scores = pl.pallas_call(
        docs_kernel,
        out_shape=jax.ShapeDtypeStruct((1, requests.shape[0]), f32),
        in_specs=[pl.BlockSpec(memory_space=pltpu.SMEM), VMEM, VMEM],
        out_specs=VMEM,
        name="docs",
    )(plan, every_vector, doc_vectors)
    return (layer_out, doc_scores)


def solution(mesh):
    placed = (
        P("wide", None),
        P(),
        P(None, None, "narrow"),
        P(None, "narrow"),
        P("narrow", None),
        P(),
        P(),
        P("wide", None),
        P("wide", None, "narrow"),
        P("wide", None, "narrow"),
        P("wide", "narrow", None),
        P(),
        P(("wide", "narrow"), None),
        P(("wide", "narrow"), None),
        P(("wide", "narrow"), None),
    )
    return jax.shard_map(
        body,
        mesh=mesh,
        in_specs=placed,
        out_specs=(P("wide", None), P(("wide", "narrow"), None)),
        check_vma=False,
    )
```

```python
import functools

import jax
import jax.numpy as jnp
from jax import lax
from jax.experimental import pallas as pl
from jax.experimental.pallas import tpu as pltpu
from jax.sharding import PartitionSpec as P

HD = 128
TOK_DEV = 128
MOST_REQ = 64
DOC_MOST = 128
LANES = 128

EPS = 1e-06
THETA = 50000.0
NEG = -1e30
MIB = 1 << 20

f32 = jnp.float32
bf16 = jnp.bfloat16
VMEM = pl.BlockSpec(memory_space=pltpu.VMEM)


def rms_norm(values, gain):
    return values * lax.rsqrt(jnp.mean(values * values, axis=-1, keepdims=True) + EPS) * gain


def request_layout(lengths_row, count):
    bounds = jnp.cumsum(lengths_row)
    places = jnp.arange(count, dtype=jnp.int32)
    member = jnp.sum((places[:, None] >= bounds[None, :-1]).astype(jnp.int32), axis=1)
    starts = bounds - lengths_row
    pick = member[:, None] == jnp.arange(lengths_row.shape[0], dtype=jnp.int32)[None, :]
    offsets = places - jnp.sum(jnp.where(pick, starts[None, :], 0), axis=1)
    return (member, offsets)


def front_kernel(tokens, gain, w_qkv, qk_gain, cosine, sine, bias, mixed, normed):
    @pl.when(pl.program_id(0) == 0)
    def _():
        normed[...] = rms_norm(tokens[...].astype(f32), gain[...]).astype(bf16)

    heads = mixed.shape[1] // HD
    parts = [jnp.dot(normed[...], w_qkv[i], preferred_element_type=f32) for i in range(3)]
    for head in range(heads):
        lanes = slice(head * HD, (head + 1) * HD)

        def turned(part):
            v = rms_norm(parts[part][:, lanes], qk_gain[part : part + 1, lanes])
            return (v * cosine[...] + pltpu.roll(v, HD // 2, 1) * sine[...]).astype(bf16)

        query, keys = turned(0), turned(1)
        values = parts[2][:, lanes].astype(bf16)
        scores = lax.dot_general(
            query, keys, (((1,), (1,)), ((), ())), preferred_element_type=f32
        ) * (HD ** (-0.5))
        scores = jnp.where(bias[...] > 0, scores, NEG)
        weights = jnp.exp(scores - jnp.max(scores, axis=-1, keepdims=True))
        probs = (weights / jnp.sum(weights, axis=-1, keepdims=True)).astype(bf16)
        mixed[:, lanes] = jnp.dot(probs, values, preferred_element_type=f32).astype(bf16)


def partner_barrier(peers):
    barrier = pltpu.get_barrier_semaphore()
    me = lax.axis_index("narrow")
    for k in range(1, peers):
        pl.semaphore_signal(
            barrier,
            inc=1,
            device_id={"narrow": (me + k) % peers},
            device_id_type=pl.DeviceIdType.MESH,
        )
    pl.semaphore_wait(barrier, peers - 1)


def send_peers(peers, src, slot, send_sem, recv_sem, piece):
    me = lax.axis_index("narrow")
    copies = []
    for k in range(1, peers):
        copy = pltpu.make_async_remote_copy(
            src_ref=src,
            dst_ref=slot(k),
            send_sem=send_sem.at[k, piece],
            recv_sem=recv_sem.at[k, piece],
            device_id={"narrow": (me + k) % peers},
            device_id_type=pl.DeviceIdType.MESH,
        )
        copy.start()
        copies.append(copy)
    return copies


def sum_peers(peers, load):
    me = lax.axis_index("narrow")
    return sum(load((me - j + peers) % peers).astype(f32) for j in range(peers))


def join_kernel(
    peers, pieces, experts, mixed, w_out, tokens, gain, w_router, routes,
    hidden, extended, parts, send_sem, recv_sem,
):
    partner_barrier(peers)
    width = w_out.shape[1]
    step = width // pieces
    copies = []
    for piece in range(pieces):
        lanes = pl.ds(piece * step, step)
        parts[0, piece] = jnp.dot(
            mixed[...], w_out[:, lanes], preferred_element_type=f32
        ).astype(bf16)
        copies.append(
            send_peers(
                peers,
                parts.at[0, piece],
                lambda k: parts.at[k, piece],
                send_sem,
                recv_sem,
                piece,
            )
        )
    total = 0.0
    for piece in range(pieces):
        lanes = pl.ds(piece * step, step)
        for copy in copies[piece]:
            copy.wait()
        attn = sum_peers(peers, lambda k: parts[k, piece])
        row = (tokens[:, lanes].astype(f32) + attn).astype(bf16)
        hidden[:, lanes] = row
        row = row.astype(f32)
        total = total + jnp.sum(row * row, axis=-1, keepdims=True)
    scale = lax.rsqrt(total / width + EPS)
    normed = (hidden[...].astype(f32) * scale * gain[...]).astype(bf16)
    extended[:, :width] = normed
    logits = jnp.dot(normed, w_router[...], preferred_element_type=f32)
    lane = lax.broadcasted_iota(jnp.int32, logits.shape, 1)
    expert = jnp.where(lane < experts, lane, lane - experts)
    routed = routes[:, 0:1] == expert
    for k in range(1, routes.shape[1]):
        routed = routed | (routes[:, k : k + 1] == expert)
    lifted = jnp.where(routed, 1.0 / (1.0 + jnp.exp(-logits)), 0.0)
    first = lane < experts
    gates = lifted / jnp.sum(jnp.where(first, lifted, 0.0), axis=-1, keepdims=True)
    high = gates.astype(bf16).astype(f32)
    extended[:, width:] = jnp.where(first, high, gates - high).astype(bf16)


def gather_kernel(depth, own, out, local_sem, z_sem, x_sem, y_sem, dx_sem, dy_sem, core_sem):
    wide, narrow = lax.axis_index("wide"), lax.axis_index("narrow")
    z, side, core = wide // 4, wide // 2 % 2, wide % 2
    share = own.shape[0]
    half = share // 2
    to_up, to_down = {"wide": wide + 4}, {"wide": wide - 4}
    to_x, to_y = {"wide": wide + 2 - 4 * side}, {"narrow": 1 - narrow}
    to_core = {"wide": wide + 1 - 2 * core}

    barrier = pltpu.get_barrier_semaphore()

    def greet(device):
        pl.semaphore_signal(
            barrier, inc=1, device_id=device, device_id_type=pl.DeviceIdType.MESH
        )

    for device in (to_x, to_y, to_core):
        greet(device)
    pl.when(z < depth - 1)(lambda: greet(to_up))
    pl.when(z > 0)(lambda: greet(to_down))
    pl.semaphore_wait(barrier, 3 + (z + depth - 1) // depth + (2 * depth - 2 - z) // depth)

    def place(s, across_x, across_y, part=None, cores=core):
        along = 1 - side if across_x else side
        lane = 1 - narrow if across_y else narrow
        at = ((s * 4 + along * 2 + cores) * 2 + lane) * share
        if part is None:
            return out.at[pl.ds(pl.multiple_of(at, 16), share)]
        return out.at[pl.ds(pl.multiple_of(at + part * half, 16), half)]

    def copy(ref, sems, index, device):
        return pltpu.make_async_remote_copy(
            src_ref=ref,
            dst_ref=ref,
            send_sem=sems.at[0, index],
            recv_sem=sems.at[1, index],
            device_id=device,
            device_id_type=pl.DeviceIdType.MESH,
        )

    def upward(s):
        return copy(place(s, 0, 0), z_sem, s, to_up)

    def downward(s):
        return copy(place(s, 0, 0), z_sem, s + depth, to_down)

    def cross(s, kind):
        return copy(place(s, kind & 1, kind >> 1), core_sem, s * 4 + kind, to_core)

    def over_x(s):
        return copy(place(s, 0, 0), x_sem, s, to_x)

    def over_y(s):
        return copy(place(s, 0, 0), y_sem, s, to_y)

    def corner_y(s):
        return copy(place(s, 1, 0, 0), dy_sem, s, to_y)

    def corner_x(s):
        return copy(place(s, 0, 1, 1), dx_sem, s, to_x)

    def first(s, up, down):
        if up:
            pl.when(z < depth - 1)(lambda: upward(s).start())
        if down:
            pl.when(z > 0)(lambda: downward(s).start())
        over_x(s).start()
        over_y(s).start()
        cross(s, 0).start()

    def second(s):
        over_x(s).wait_recv()
        corner_y(s).start()
        cross(s, 1).start()
        over_y(s).wait_recv()
        corner_x(s).start()
        cross(s, 2).start()

    def third(s):
        corner_y(s).wait_recv()
        corner_x(s).wait_recv()
        cross(s, 3).start()

    def at_distance(d, do):
        if d == 0:
            do(z, True, True)
            return
        pl.when(z >= d)(lambda: do(z - d, True, False))
        pl.when(z + d < depth)(lambda: do(z + d, False, True))

    def begin(s, up, down):
        if not (up and down):
            (upward(s) if up else downward(s)).wait_recv()
        first(s, up, down)

    keep = pltpu.make_async_copy(own, place(z, 0, 0), local_sem)
    keep.start()
    keep.wait()
    for d in range(depth + 2):
        if d < depth:
            at_distance(d, begin)
        if 0 <= d - 1 < depth:
            at_distance(d - 1, lambda s, up, down: second(s))
        if 0 <= d - 2:
            at_distance(d - 2, lambda s, up, down: third(s))

    def finish(s, up, down):
        if up:
            pl.when(z < depth - 1)(lambda: upward(s).wait_send())
        if down:
            pl.when(z > 0)(lambda: downward(s).wait_send())
        for done in (over_x(s), over_y(s), corner_x(s), corner_y(s)):
            done.wait_send()
        for kind in range(4):
            cross(s, kind).wait()

    for d in range(depth):
        at_distance(d, finish)


def gather(own, identity, name):
    if lax.axis_size("narrow") != 2 or lax.axis_size("wide") % 4:
        return lax.all_gather(own, ("wide", "narrow"), axis=0, tiled=True)
    devices = lax.axis_size("wide") * lax.axis_size("narrow")
    depth = lax.axis_size("wide") // 4
    pair = pltpu.SemaphoreType.DMA((2, depth))
    return pl.pallas_call(
        functools.partial(gather_kernel, depth),
        out_shape=jax.ShapeDtypeStruct((devices * own.shape[0], own.shape[1]), own.dtype),
        in_specs=[pl.BlockSpec(memory_space=pl.ANY)],
        out_specs=pl.BlockSpec(memory_space=pl.ANY),
        scratch_shapes=[
            pltpu.SemaphoreType.DMA,
            pltpu.SemaphoreType.DMA((2, 2 * depth)),
            pair,
            pair,
            pair,
            pair,
            pltpu.SemaphoreType.DMA((2, 4 * depth)),
        ],
        compiler_params=pltpu.CompilerParams(collective_id=identity, has_side_effects=True),
        name=name,
    )(own)


def moe_kernel(rows, chosen, w_gate, w_up, w_down, out):
    width = out.shape[1]
    block = rows[...].reshape(out.shape[0], rows.shape[2])
    x = block[:, :width]
    table = block[:, width:].astype(f32)
    total = 0.0
    for e in range(w_gate.shape[0]):
        gate = jnp.sum(table * chosen[e : e + 1, :], axis=-1, keepdims=True)
        lift = jnp.dot(x, w_gate[e], preferred_element_type=f32)
        upward = jnp.dot(x, w_up[e], preferred_element_type=f32)
        active = (lift / (1.0 + jnp.exp(-lift)) * upward * gate).astype(bf16)
        total = total + jnp.dot(active, w_down[e], preferred_element_type=f32)
    out[...] = total.astype(bf16)


def tail_kernel(
    peers, pieces, partial_out, hidden, gain, w_proj,
    layer_out, vectors, theirs, send_sem, recv_sem,
):
    partner_barrier(peers)
    step = hidden.shape[0] // pieces
    copies = []
    for piece in range(pieces):
        rows = pl.ds(piece * step, step)
        copies.append(
            send_peers(
                peers,
                partial_out.at[rows],
                lambda k: theirs.at[k, rows],
                send_sem,
                recv_sem,
                piece,
            )
        )
    theirs[0] = partial_out[...]
    for piece in range(pieces):
        rows = pl.ds(piece * step, step)
        for copy in copies[piece]:
            copy.wait()
        moe = sum_peers(peers, lambda k: theirs[k, rows, :])
        out = (hidden[rows, :].astype(f32) + moe).astype(bf16)
        layer_out[rows, :] = out
        normed = rms_norm(out.astype(f32), gain[...]).astype(bf16)
        embedded = jnp.dot(normed, w_proj[...], preferred_element_type=f32)
        vectors[rows, :] = (
            embedded * lax.rsqrt(jnp.sum(embedded * embedded, axis=-1, keepdims=True) + EPS)
        ).astype(bf16)


def docs_kernel(plan, vectors, docs, scores):
    held = scores.shape[1]
    q_rows = MOST_REQ + 16
    d_rows = DOC_MOST + 128
    lane = lax.broadcasted_iota(jnp.int32, (1, held), 1)
    row = lax.broadcasted_iota(jnp.int32, (q_rows, 1), 0)
    column = lax.broadcasted_iota(jnp.int32, (1, d_rows), 1)
    out = jnp.zeros((1, held), f32)
    for doc in range(held):
        q_first, q_size = plan[0, doc], plan[1, doc]
        d_first, d_size = plan[2, doc], plan[3, doc]
        q_at = pl.multiple_of(jnp.minimum(q_first // 16 * 16, vectors.shape[0] - q_rows), 16)
        d_at = pl.multiple_of(jnp.minimum(d_first // 16 * 16, docs.shape[0] - d_rows), 16)
        sims = lax.dot_general(
            vectors[pl.ds(q_at, q_rows), :],
            docs[pl.ds(d_at, d_rows), :],
            (((1,), (1,)), ((), ())),
            preferred_element_type=f32,
        )
        place = column + d_at
        sims = jnp.where((place >= d_first) & (place < d_first + d_size), sims, NEG)
        best = jnp.max(sims, axis=1, keepdims=True)
        place = row + q_at
        best = jnp.where((place >= q_first) & (place < q_first + q_size), best, 0.0)
        total = jnp.sum(best, axis=0, keepdims=True) / q_size.astype(f32)
        out = jnp.where(lane == doc, total, out)
    scores[...] = out


def body(
    tokens,
    request_lengths,
    w_qkv,
    qk_gain,
    w_out,
    norm_gains,
    w_router,
    routes,
    w_gate,
    w_up,
    w_down,
    w_proj,
    doc_vectors,
    doc_segment,
    doc_request,
):
    count, width = tokens.shape
    experts = w_router.shape[1]
    experts_here = w_gate.shape[0]
    columns = w_qkv.shape[2]
    shards = request_lengths.shape[0]
    wide = lax.axis_index("wide")
    narrow = lax.axis_index("narrow")
    peers = lax.axis_size("narrow")

    lengths_row = lax.dynamic_slice_in_dim(request_lengths, wide, 1, 0)[0]
    member, offsets = request_layout(lengths_row, count)
    half = HD // 2
    freq = THETA ** (-jnp.arange(half, dtype=f32) / half)
    angle = offsets.astype(f32)[:, None] * freq[None, :]
    cosine, sine = jnp.cos(angle), jnp.sin(angle)
    cosine = jnp.concatenate([cosine, cosine], axis=1)
    sine = jnp.concatenate([-sine, sine], axis=1)
    same = (member[:, None] == member[None, :]).astype(f32)

    block = 256
    mixed = pl.pallas_call(
        front_kernel,
        out_shape=jax.ShapeDtypeStruct((count, columns), bf16),
        grid=(columns // block,),
        in_specs=[
            pl.BlockSpec((count, width), lambda i: (0, 0)),
            pl.BlockSpec((1, width), lambda i: (0, 0)),
            pl.BlockSpec((3, width, block), lambda i: (0, 0, i)),
            pl.BlockSpec((2, block), lambda i: (0, i)),
            pl.BlockSpec((count, HD), lambda i: (0, 0)),
            pl.BlockSpec((count, HD), lambda i: (0, 0)),
            pl.BlockSpec((count, count), lambda i: (0, 0)),
        ],
        out_specs=pl.BlockSpec((count, block), lambda i: (0, i)),
        scratch_shapes=[pltpu.VMEM((count, width), bf16)],
        compiler_params=pltpu.CompilerParams(vmem_limit_bytes=24 * MIB),
        name="front",
    )(tokens, norm_gains[0:1], jnp.transpose(w_qkv, (1, 0, 2)), qk_gain, cosine, sine, same)

    extra = (2 * experts + LANES - 1) // LANES * LANES
    routers = jnp.concatenate(
        [w_router, w_router, jnp.zeros((width, extra - 2 * experts), bf16)], axis=1
    )
    pieces = 4
    hidden, extended = pl.pallas_call(
        functools.partial(join_kernel, peers, pieces, experts),
        out_shape=(
            jax.ShapeDtypeStruct((count, width), bf16),
            jax.ShapeDtypeStruct((count, width + extra), bf16),
        ),
        in_specs=[VMEM] * 6,
        out_specs=(VMEM, VMEM),
        scratch_shapes=[
            pltpu.VMEM((peers, pieces, count, width // pieces), bf16),
            pltpu.SemaphoreType.DMA((peers, pieces)),
            pltpu.SemaphoreType.DMA((peers, pieces)),
        ],
        compiler_params=pltpu.CompilerParams(
            collective_id=0, has_side_effects=True, vmem_limit_bytes=24 * MIB
        ),
        name="join",
    )(mixed, w_out, tokens, norm_gains[1:2], routers, routes)

    share = count // peers
    own_rows = lax.dynamic_slice_in_dim(extended, narrow * share, share, 0)
    rows = gather(own_rows, 2, "gather_rows")

    ids = wide * experts_here + jnp.arange(experts_here, dtype=jnp.int32)
    lane = jnp.arange(extra, dtype=jnp.int32)[None, :]
    chosen = ((lane == ids[:, None]) | (lane == ids[:, None] + experts)).astype(f32)
    halves = 2
    depth = count // halves
    view = rows.reshape(shards, halves, depth, width + extra)
    group = 4
    scattered = []
    for part in range(halves):
        partial_out = pl.pallas_call(
            moe_kernel,
            out_shape=jax.ShapeDtypeStruct((shards * depth, width), bf16),
            grid=(shards // group,),
            in_specs=[
                pl.BlockSpec(
                    (group, None, depth, width + extra), lambda i, part=part: (i, part, 0, 0)
                ),
                pl.BlockSpec(chosen.shape, lambda i: (0, 0)),
                pl.BlockSpec(w_gate.shape, lambda i: (0, 0, 0)),
                pl.BlockSpec(w_up.shape, lambda i: (0, 0, 0)),
                pl.BlockSpec(w_down.shape, lambda i: (0, 0, 0)),
            ],
            out_specs=pl.BlockSpec((group * depth, width), lambda i: (i, 0)),
            compiler_params=pltpu.CompilerParams(vmem_limit_bytes=48 * MIB),
            cost_estimate=pl.CostEstimate(
                flops=6 * shards * depth * w_gate.size,
                bytes_accessed=6 * w_gate.size + 4 * shards * depth * width,
                transcendentals=0,
            ),
            name="experts",
        )(view, chosen, w_gate, w_up, w_down)
        scattered.append(lax.psum_scatter(partial_out, "wide", scatter_dimension=0, tiled=True))
    scattered = jnp.concatenate(scattered, axis=0)

    pieces = 4
    layer_out, vectors = pl.pallas_call(
        functools.partial(tail_kernel, peers, pieces),
        out_shape=(
            jax.ShapeDtypeStruct((count, width), bf16),
            jax.ShapeDtypeStruct((count, w_proj.shape[1]), bf16),
        ),
        in_specs=[VMEM] * 4,
        out_specs=(VMEM, VMEM),
        scratch_shapes=[
            pltpu.VMEM((peers, count, width), bf16),
            pltpu.SemaphoreType.DMA((peers, pieces)),
            pltpu.SemaphoreType.DMA((peers, pieces)),
        ],
        compiler_params=pltpu.CompilerParams(
            collective_id=1, has_side_effects=True, vmem_limit_bytes=24 * MIB
        ),
        name="tail",
    )(scattered, hidden, norm_gains[2:3], w_proj)

    own_vectors = lax.dynamic_slice_in_dim(vectors, narrow * share, share, 0)
    every_vector = gather(own_vectors, 3, "gather_vectors")

    flat_lengths = request_lengths.reshape(-1)
    starts = jnp.cumsum(request_lengths, axis=1) - request_lengths
    flat_starts = (starts + TOK_DEV * jnp.arange(shards, dtype=jnp.int32)[:, None]).reshape(-1)
    requests = doc_request[0]
    pick = requests[:, None] == jnp.arange(flat_lengths.shape[0], dtype=jnp.int32)[None, :]
    docs = jnp.arange(requests.shape[0], dtype=jnp.int32)[:, None]
    plan = jnp.stack(
        [
            jnp.sum(jnp.where(pick, flat_starts[None, :], 0), axis=1),
            jnp.sum(jnp.where(pick, flat_lengths[None, :], 0), axis=1),
            jnp.sum((doc_segment < docs).astype(jnp.int32), axis=1),
            jnp.sum((doc_segment == docs).astype(jnp.int32), axis=1),
        ]
    )
    doc_scores = pl.pallas_call(
        docs_kernel,
        out_shape=jax.ShapeDtypeStruct((1, requests.shape[0]), f32),
        in_specs=[pl.BlockSpec(memory_space=pltpu.SMEM), VMEM, VMEM],
        out_specs=VMEM,
        name="docs",
    )(plan, every_vector, doc_vectors)
    return (layer_out, doc_scores)


def solution(mesh):
    placed = (
        P("wide", None),
        P(),
        P(None, None, "narrow"),
        P(None, "narrow"),
        P("narrow", None),
        P(),
        P(),
        P("wide", None),
        P("wide", None, "narrow"),
        P("wide", None, "narrow"),
        P("wide", "narrow", None),
        P(),
        P(("wide", "narrow"), None),
        P(("wide", "narrow"), None),
        P(("wide", "narrow"), None),
    )
    return jax.shard_map(
        body,
        mesh=mesh,
        in_specs=placed,
        out_specs=(P("wide", None), P(("wide", "narrow"), None)),
        check_vma=False,
    )
```
